32 devices in a mesh: grp: 2 (over y), row: 4 (over x, core), col: 4 (over z).
Axes of the slice: x: 2, y: 2, z: 4, core: 2. Of those that a mesh axis runs over, the one named last changes fastest.
Arguments:
- density: float32 [32, 4, 2, 128, 128], P(('grp', 'row'), 'col'), parts along dimension 0, as said below
- slot_cols: int32 [32, 4, 2], P('grp'), parts along dimension 0, may hold values from -1 to 15, as said below
- block_at: int32 [32], P('grp'), parts along dimension 0, may hold values from 0 to 15, as said below
Outputs:
- purified: float32 [32, 4, 2, 128, 128], P(('grp', 'row'), 'col'), parts along dimension 0
The draws below stay inside these ranges and needn't reach their ends.
There are 2 independent parts, one for each index of `grp`. The reference program is written for one: setup_inputs(seed, part) draws one part's arguments, and reference() takes and returns one part's arrays. A program takes and returns all parts, laid end to end along the dimension named above; each array names one. Nothing has to cross between parts.
Inputs may be any that keep to these rules, and one draw needn't show every extreme that they name: block_at is a permutation of the 16 block ids; position p of a block fixes the device along `row` that holds its block row (p // 4) and the column group of its block column (p // 4). slot_cols[p, c, u] is -1 or the id of a block whose position lies in column group c; in each row and group the live slots come first and name distinct blocks; slot 0 of a row in its own group is the row's own block; the pattern is symmetric: block j is stored in the row of block i exactly when block i is stored in the row of block j. `density`: the tile in slot (p, c, u) is block (block_at[p], slot_cols[p, c, u]) of a symmetric matrix, so the stored tile of block (j, i) is its transpose; tiles of empty slots are zero.
All inputs are finite; a program needn't handle non-finite values.
Results may differ from the reference program's by a relative error of at most 0.0003.
Values sent between devices are 32-bit elements; how exact they have to be, the bound alone decides.
A program may use at most 128 MiB of HBM per device.

```python
import jax
import jax.numpy as jnp
from jax import lax

BLK = 128
WC = 2
NB = 16
N_COL = 4


def layout(key):
    key_perm, key_count, key_shift, key_order = jax.random.split(key, 4)
    block_at = jax.random.permutation(key_perm, NB).astype(jnp.int32)
    group_span = NB // N_COL
    group_ids = jnp.arange(N_COL, dtype=jnp.int32)
    upper_pair = group_ids[:, None] < group_ids[None, :]
    diag_pair = group_ids[:, None] == group_ids[None, :]
    raw_counts = jax.random.randint(key_count, (N_COL, N_COL), 0, WC + 1).astype(jnp.int32)
    counts = jnp.where(upper_pair, raw_counts, raw_counts.T)
    counts = jnp.where(diag_pair, WC, counts).astype(jnp.int32)
    raw_shifts = jax.random.randint(key_shift, (N_COL, N_COL), 0, group_span).astype(jnp.int32)
    shifts = jnp.where(upper_pair, raw_shifts, raw_shifts.T)
    order_keys = jax.random.split(key_order, N_COL * N_COL)
    orders = jax.vmap(lambda one_key: jax.random.permutation(one_key, group_span))(order_keys)
    orders = orders.reshape(N_COL, N_COL, group_span).astype(jnp.int32)
    orders = jnp.where(upper_pair[..., None], orders, jnp.transpose(orders, (1, 0, 2)))
    inverse = jnp.argsort(orders, axis=-1).astype(jnp.int32)
    grid_pos = jnp.arange(NB, dtype=jnp.int32)[:, None, None]
    row_group = grid_pos // group_span
    inside = grid_pos % group_span
    col_group = group_ids[None, :, None]
    slot_ids = jnp.arange(WC, dtype=jnp.int32)[None, None, :]
    order_pick = orders[row_group[:, :, 0], col_group[:, :, 0]]
    inverse_pick = inverse[row_group[:, :, 0], col_group[:, :, 0]]
    shift_pick = shifts[row_group[:, :, 0], col_group[:, :, 0]][..., None]
    count_pick = counts[row_group[:, :, 0], col_group[:, :, 0]][..., None]
    inside_full = jnp.broadcast_to(inside, (NB, N_COL, 1))
    inside_inverse = jnp.take_along_axis(inverse_pick, inside_full, axis=-1)
    diag_index = (inside_inverse + slot_ids * (group_span // 2)) % group_span
    diag_col = jnp.take_along_axis(order_pick, diag_index, axis=-1)
    upper_index = (inside + shift_pick + slot_ids) % group_span
    upper_col = jnp.take_along_axis(order_pick, upper_index, axis=-1)
    lower_col = (inside_inverse - shift_pick - slot_ids) % group_span
    chosen_col = jnp.where(row_group == col_group, diag_col, jnp.where(row_group < col_group, upper_col, lower_col))
    is_live = slot_ids < count_pick
    cols_pos = jnp.where(is_live, col_group * group_span + chosen_col, -1).astype(jnp.int32)
    return (block_at, cols_pos)


def draw_slot_cols(key, part):
    block_at, cols_pos = layout(key)
    named = block_at[jnp.maximum(cols_pos, 0)]
    return jnp.where(cols_pos >= 0, named, -1).astype(jnp.int32)


def draw_block_at(key, part):
    block_at, cols_pos = layout(key)
    return block_at


def draw_density(key, part):
    block_at, cols_pos = layout(key)
    key = jax.random.fold_in(key, 7)
    row_pos = jnp.broadcast_to(jnp.arange(NB, dtype=jnp.int32)[:, None, None], cols_pos.shape)
    col_pos = jnp.maximum(cols_pos, 0)
    lower_pos = jnp.minimum(row_pos, col_pos)
    higher_pos = jnp.maximum(row_pos, col_pos)
    pair_ids = (lower_pos * NB + higher_pos).reshape(-1)
    spread = 0.7 / (BLK * N_COL * WC) ** 0.5

    def make_tile(pair_id):
        tile_key = jax.random.fold_in(key, pair_id)
        values = jax.random.truncated_normal(tile_key, -4.0, 4.0, (BLK, BLK), jnp.float32)
        return values * spread
    tiles = jax.vmap(make_tile)(pair_ids).reshape(NB, N_COL, WC, BLK, BLK)
    flipped = jnp.swapaxes(tiles, -1, -2)
    identity = jnp.eye(BLK, dtype=jnp.float32)
    diagonal_tile = (tiles + flipped) * 0.7071 + 0.5 * identity
    row_b = row_pos[..., None, None]
    col_b = col_pos[..., None, None]
    result = jnp.where(row_b == col_b, diagonal_tile, jnp.where(row_b < col_b, tiles, flipped))
    result = jnp.where((cols_pos >= 0)[..., None, None], result, 0.0)
    return result.astype(jnp.float32)


def setup_inputs(seed: int = 0, part: int = 0) -> dict:
    keys = jax.random.split(jax.random.key(seed), 4)
    part_keys = jax.random.split(jax.random.fold_in(keys[3], part), 4)
    return {
        "density": draw_density(jax.random.fold_in(jax.random.fold_in(keys[3], part), 71), part),
        "slot_cols": draw_slot_cols(jax.random.fold_in(jax.random.fold_in(keys[3], part), 71), part),
        "block_at": draw_block_at(jax.random.fold_in(jax.random.fold_in(keys[3], part), 71), part),
    }


HIGHEST = lax.Precision.HIGHEST


def positions(block_at, block_ids):
    nblocks = block_at.shape[0]
    order_ids = jnp.arange(nblocks, dtype=jnp.int32)
    return jnp.max(jnp.where(block_at == block_ids[..., None], order_ids, 0), axis=-1).astype(jnp.int32)


def star(left_side, right_side, slot_cols, block_at):
    nblocks, ngroups, slot_count = slot_cols.shape
    targets = positions(block_at, slot_cols)
    group_ids = jnp.arange(ngroups, dtype=jnp.int32)
    slot_ids = jnp.arange(slot_count, dtype=jnp.int32)

    def one_row(position):
        row_ids = slot_cols[position]
        is_live = row_ids >= 0
        target_pos = targets[position]
        candidates = slot_cols[target_pos]
        matches = (candidates[:, :, :, None, :] == row_ids[None, None, :, :, None])
        matches = matches & is_live[None, None, :, :, None] & is_live[:, :, None, None, None]
        present = jnp.any(matches, axis=-1)
        chosen_slot = jnp.max(jnp.where(matches, slot_ids, 0), axis=-1).astype(jnp.int32)
        selected = right_side[target_pos[:, :, None, None], group_ids[None, None, :, None], chosen_slot]
        selected = jnp.where(present[..., None, None], selected, jnp.zeros_like(selected))
        return jnp.einsum('kvab,cukvdb->cuad', left_side[position], selected, precision=HIGHEST)

    return lax.map(one_row, jnp.arange(nblocks, dtype=jnp.int32))


def reference(density, slot_cols, block_at):
    square = star(density, density, slot_cols, block_at)
    correction = star(square, density, slot_cols, block_at) + star(density, square, slot_cols, block_at)
    return 3.0 * square - correction
```

```python
import functools
import heapq

import jax
import jax.numpy as jnp
from jax import lax
from jax.experimental import pallas as pl
from jax.experimental.pallas import tpu as pltpu
from jax.sharding import PartitionSpec as P

HIGHEST = lax.Precision.HIGHEST


def positions(block_at, block_ids):
    nblocks = block_at.shape[0]
    order_ids = jnp.arange(nblocks, dtype=jnp.int32)
    return jnp.max(jnp.where(block_at == block_ids[..., None], order_ids, 0), axis=-1)


def on_device(density, slot_cols, block_at):
    row_count, _, slot_count, tile_size, _ = density.shape
    nblocks, ngroups, _ = slot_cols.shape
    first_row = lax.axis_index("row") * row_count
    my_group = lax.axis_index("col")
    my_cols = lax.dynamic_slice_in_dim(slot_cols, first_row, row_count, 0)
    is_live = my_cols >= 0
    target_pos = positions(block_at, my_cols)
    own_ids = lax.dynamic_index_in_dim(my_cols, my_group, 1, keepdims=False)
    panel_ids = lax.dynamic_index_in_dim(slot_cols, my_group, 1, keepdims=False)
    slot_ids = jnp.arange(slot_count, dtype=jnp.int32)
    candidates = panel_ids[target_pos]
    matches = candidates[:, :, :, None, :] == own_ids[:, None, None, :, None]
    matches = matches & (own_ids >= 0)[:, None, None, :, None] & is_live[:, :, :, None, None]
    present = jnp.any(matches, axis=-1)
    chosen_slot = jnp.max(jnp.where(matches, slot_ids, 0), axis=-1)
    flat_index = target_pos[..., None] * slot_count + chosen_slot
    own_tiles = density[:, 0]

    def slot_terms(left_side, flat_panel, group_count):
        summed = jnp.zeros((group_count, row_count, slot_count, tile_size, tile_size), jnp.float32)
        for kslot in range(slot_count):
            selected = jnp.take(flat_panel, flat_index[..., kslot], axis=0)
            selected = jnp.where(present[..., kslot, None, None], selected, 0.0)
            summed = summed + jnp.einsum(
                "pab,pcudb->cpuad", left_side[:, kslot], selected, precision=HIGHEST
            )
        return summed

    gathered = lax.all_gather(density, "row", axis=0, tiled=True)
    flat_density = gathered.reshape(nblocks * slot_count, tile_size, tile_size)
    square_part = lax.psum_scatter(
        slot_terms(own_tiles, flat_density, lax.axis_size("col") * 1),
        "col",
        scatter_dimension=0,
        tiled=True,
    )
    square = square_part.reshape(row_count, slot_count, tile_size, tile_size)
    square_gathered = lax.all_gather(square, "row", axis=0, tiled=True)
    flat_square = square_gathered.reshape(nblocks * slot_count, tile_size, tile_size)
    cubic_part = lax.psum_scatter(
        slot_terms(square, flat_density, lax.axis_size("col") * 1)
        + slot_terms(own_tiles, flat_square, lax.axis_size("col") * 1),
        "col",
        scatter_dimension=0,
        tiled=True,
    )
    purified = 3.0 * square - cubic_part.reshape(row_count, slot_count, tile_size, tile_size)
    return purified.reshape(row_count, 1, slot_count, tile_size, tile_size)


SIDE = 4
PAIRS = tuple((i, j) for i in range(SIDE) for j in range(i, SIDE))
PARENTS = (
    (0, 0, 1, 2, 0, 4, 5, 6), (0, 1, 1, 2, 0, 1, 5, 3), (4, 0, 2, 7, 4, 4, 2, 6),
    (4, 2, 3, 3, 4, 4, 7, 3), (1, 1, 1, 2, 5, 1, 5, 6), (1, 2, 2, 2, 0, 5, 2, 3),
    (1, 5, 3, 3, 0, 5, 2, 3), (4, 2, 6, 7, 5, 6, 6, 6), (4, 5, 3, 7, 5, 6, 6, 7),
    (1, 5, 6, 7, 5, 6, 7, 7),
)
MESH = pl.DeviceIdType.MESH
NT = (((1,), (1,)), ((), ()))


def orientation(pair, chip):
    while PARENTS[pair][chip] != chip:
        chip = PARENTS[pair][chip]
    i, j = PAIRS[pair]
    return (i, j) if (i // 2) * SIDE + j == chip else (j, i)


def make_plan():
    heap, free, count = [], {}, 0
    plan = {(r, c): [] for r in range(SIDE) for c in range(SIDE)}

    def children(pair, chip):
        return [k for k in range(8) if k != chip and PARENTS[pair][k] == chip]

    def below(pair, chip):
        return 1 + max([below(pair, k) for k in children(pair, chip)], default=0)

    for pair in range(len(PAIRS)):
        for chip in range(8):
            if PARENTS[pair][chip] == chip:
                i, j = orientation(pair, chip)
                for row in range(SIDE):
                    heap.append((0.0, row, -below(pair, chip), count, pair, (i, j), None))
                    count += 1
    heapq.heapify(heap)
    while heap:
        now, row, _, _, pair, dev, source = heapq.heappop(heap)
        chip = (dev[0] // 2) * SIDE + dev[1]
        i, j = orientation(pair, chip)
        targets = []
        if source is None or dev[0] % 2 == i % 2:
            for k in sorted(children(pair, chip), key=lambda k: -below(pair, k)):
                targets.append((((k // SIDE) * 2 + i % 2, k % SIDE), (chip, k), 1.35))
            targets.append(((dev[0] ^ 1, dev[1]), dev, 0.3))
        plan[dev].append((i * SIDE + j, row, source, tuple(t[0] for t in targets)))
        for target, link, cost in targets:
            done = max(now, free.get(link, 0.0)) + cost
            free[link] = done
            heapq.heappush(heap, (done + 1.0, row, 0, count, pair, target, dev))
            count += 1
    return plan


def split(value):
    high = value.astype(jnp.bfloat16)
    return high, (value - high.astype(jnp.float32)).astype(jnp.bfloat16)


def purify_kernel(plan, targets, lookup, mine, out, held, high, low, s32, s_high, s_low, send_sem, recv_sem, own_sem):
    r, c = lax.axis_index("row"), lax.axis_index("col")
    chip = (r // 2) * SIDE + c
    zero = high.shape[0] - 1
    s_zero = s_high.shape[0] - 1

    def greet(row, col):
        pl.semaphore_signal(barrier, inc=1, device_id={"row": row, "col": col}, device_id_type=MESH)

    barrier = pltpu.get_barrier_semaphore()
    greet(r + 1 - 2 * (r % 2), c)
    greet((r + 2) % SIDE, c)

    @pl.when(c > 0)
    def _():
        greet(r, c - 1)

    @pl.when(c < SIDE - 1)
    def _():
        greet(r, c + 1)

    edges = (c == 0).astype(jnp.int32) + (c == SIDE - 1).astype(jnp.int32)
    pl.semaphore_wait(barrier, 4 - edges)

    def remote(slot, row, source, target, number):
        src = mine if source is None else held.at[slot]
        return pltpu.make_async_remote_copy(
            src_ref=src.at[row],
            dst_ref=held.at[slot, row],
            send_sem=send_sem.at[number],
            recv_sem=recv_sem.at[slot, row],
            device_id={"row": target[0], "col": target[1]},
            device_id_type=MESH,
        )

    def on_each_device(action):
        for dev, steps in plan.items():
            @pl.when((r == dev[0]) & (c == dev[1]))
            def _():
                number = 0
                for slot, row, source, to in steps:
                    if action == "run" and source is not None:
                        remote(slot, row, source, source, 0).wait_recv()
                    for target in to:
                        copy = remote(slot, row, source, target, number)
                        number += 1
                        if action == "run":
                            copy.start()
                        else:
                            copy.wait_send()

    own = pltpu.make_async_copy(mine, held.at[r * SIDE + c], own_sem)
    own.start()
    high[zero] = jnp.zeros_like(high[zero])
    low[zero] = jnp.zeros_like(low[zero])
    s_high[s_zero] = jnp.zeros_like(high[zero])
    s_low[s_zero] = jnp.zeros_like(high[zero])
    on_each_device("run")
    own.wait()

    for pair, (i, j) in enumerate(PAIRS):
        turned = 0
        for k in range(8):
            if orientation(pair, k) != (i, j):
                turned = turned + (chip == k).astype(jnp.int32)
        first = i + turned * (j - i)
        second = j - turned * (j - i)

        @pl.loop(0, SIDE)
        def _(row):
            for v in range(2):
                tile = held[first * SIDE + second, row, v]
                at = ((first * SIDE + row) * SIDE + second) * 2 + v
                high[at], low[at] = split(tile)

        if i != j:
            @pl.loop(0, SIDE)
            def _(row):
                p = second * SIDE + row
                for v in range(2):
                    at = (p * SIDE + first) * 2 + v
                    source = lookup[targets[at] * 17 + p]
                    high[at] = high[source].T
                    low[at] = low[source].T

    def product(x_high, x_low, w_high, w_low):
        dot = functools.partial(lax.dot_general, dimension_numbers=NT, preferred_element_type=jnp.float32)
        return dot(x_high, w_high) + dot(x_low, w_high) + dot(x_high, w_low)

    def wide(ref, at):
        return jnp.concatenate([ref[at], ref[at + 1]], axis=1)

    def gathered(ref, index):
        return jnp.concatenate(
            [jnp.concatenate([ref[a] for a in row], axis=1) for row in index], axis=0
        )

    def rhs_index(p, group, k):
        tile = (p * SIDE + group) * 2
        ends = [targets[(p * SIDE + k) * 2 + v] for v in range(2)]
        return [[lookup[targets[tile + u] * 17 + e] for e in ends] for u in range(2)]

    @pl.loop(0, 8 * SIDE)
    def _(step):
        line, group = step // SIDE, step % SIDE
        second = line // SIDE
        p = (r + second * (c - r)) * SIDE + line % SIDE
        total = jnp.zeros((128, 256), jnp.float32)
        for k in range(SIDE):
            index = rhs_index(p, group, k)
            x = (p * SIDE + k) * 2
            total += product(wide(high, x), wide(low, x), gathered(high, index), gathered(low, index))
        for u in range(2):
            at = step * 2 + u
            tile = total[:, u * 128:(u + 1) * 128]
            s32[at] = tile
            s_high[at], s_low[at] = split(tile)

    @pl.loop(0, SIDE)
    def _(line):
        p = r * SIDE + line
        total = jnp.zeros((128, 256), jnp.float32)
        for k in range(SIDE):
            index = rhs_index(p, c, k)
            x = (line * SIDE + k) * 2
            total += product(wide(s_high, x), wide(s_low, x), gathered(high, index), gathered(low, index))
            index = [[jnp.where(a == zero, s_zero, jnp.clip(a - c * 32 + 32, 0, s_zero)) for a in row] for row in index]
            x = (p * SIDE + k) * 2
            total += product(wide(high, x), wide(low, x), gathered(s_high, index), gathered(s_low, index))
        for u in range(2):
            out[line, 0, u] = 3.0 * s32[(line * SIDE + c) * 2 + u] - total[:, u * 128:(u + 1) * 128]

    on_each_device("drain")


def on_small_grid(density, slot_cols, block_at):
    nblocks = slot_cols.shape[0]
    tiles = nblocks * SIDE * 2
    order = jnp.arange(nblocks, dtype=jnp.int32)
    flat = slot_cols.reshape(nblocks, SIDE * 2)
    targets = jnp.min(jnp.where(flat[..., None] == block_at, order, nblocks), axis=-1)
    numbers = jnp.arange(tiles, dtype=jnp.int32).reshape(nblocks, SIDE * 2)
    same = flat[:, None, :] == block_at[None, :, None]
    lookup = jnp.min(jnp.where(same, numbers[:, None, :], tiles), axis=-1)
    lookup = jnp.pad(lookup, ((0, 1), (0, 1)), constant_values=tiles)
    tile_shape = (128, 128)
    return pl.pallas_call(
        functools.partial(purify_kernel, make_plan()),
        out_shape=jax.ShapeDtypeStruct(density.shape, jnp.float32),
        in_specs=[
            pl.BlockSpec(memory_space=pltpu.SMEM),
            pl.BlockSpec(memory_space=pltpu.SMEM),
            pl.BlockSpec(memory_space=pltpu.VMEM),
        ],
        out_specs=pl.BlockSpec(memory_space=pltpu.VMEM),
        scratch_shapes=[
            pltpu.VMEM((16, SIDE, 2) + tile_shape, jnp.float32),
            pltpu.VMEM((tiles + 1,) + tile_shape, jnp.bfloat16),
            pltpu.VMEM((tiles + 1,) + tile_shape, jnp.bfloat16),
            pltpu.VMEM((64,) + tile_shape, jnp.float32),
            pltpu.VMEM((65,) + tile_shape, jnp.bfloat16),
            pltpu.VMEM((65,) + tile_shape, jnp.bfloat16),
            pltpu.SemaphoreType.DMA((64,)),
            pltpu.SemaphoreType.DMA((16, SIDE)),
            pltpu.SemaphoreType.DMA,
        ],
        compiler_params=pltpu.CompilerParams(
            collective_id=0, has_side_effects=True, vmem_limit_bytes=48 * 2**20
        ),
        cost_estimate=pl.CostEstimate(flops=7 * 10**9, bytes_accessed=2**20, transcendentals=0),
    )(targets.reshape(-1), lookup.reshape(-1), density.reshape(SIDE, 2, *tile_shape)).reshape(density.shape)


def solution(mesh):
    in_specs = (P(("grp", "row"), "col", None, None, None), P("grp", None, None), P("grp"))
    out_specs = P(("grp", "row"), "col", None, None, None)
    small = mesh.shape["row"] == SIDE and mesh.shape["col"] == SIDE
    return jax.shard_map(
        on_small_grid if small else on_device,
        mesh=mesh,
        in_specs=in_specs,
        out_specs=out_specs,
        check_vma=False,
    )
```
